128 devices in a mesh: row: 16 (over x_lo, z, core), col: 8 (over x_hi, y).
Axes of the slice: x: 4 (x_hi: 2, x_lo: 2; x = x_hi * 2 + x_lo), y: 4, z: 4, core: 2. Of those that a mesh axis runs over, the one named last changes fastest.
Arguments:
- tile_values: bfloat16 [16, 8, 384, 128, 128], P('row', 'col'), may hold values from -0.078125 to 0.078125
- tile_rows: int32 [16, 8, 384], P('row', 'col'), may hold values from 0 to 63
- tile_cols: int32 [16, 8, 384], P('row', 'col'), may hold values from 0 to 127
- tile_counts: int32 [16, 8], P('row', 'col'), may hold values from 96 to 384, as said below
- out_grad: bfloat16 [131072, 256], P(('row', 'col')), may hold values from -6 to 6
- features: bfloat16 [131072, 256], P(('row', 'col')), may hold values from -6 to 6
- weight: bfloat16 [256, 256], replicated, may hold values from -0.375 to 0.375
Outputs:
- feat_grad: bfloat16 [131072, 256], P(('row', 'col'))
- weight_grad: float32 [256, 256], replicated
The draws below stay inside these ranges and needn't reach their ends.
Inputs may be any that keep to these rules, and one draw needn't show every extreme that they name: `tile_counts`: at least one device uses all 384 slots in every draw.
All inputs are finite; a program needn't handle non-finite values.
Results may differ from the reference program's by a relative error of at most 0.015.
Values may be sent and summed in bfloat16 or wider, within the bound.
A program may use at most 256 MiB of HBM per device.

```python
import jax
import jax.numpy as jnp
from jax import lax

FEAT = 256
HIDDEN_SIZE = 256
TILE = 128
SLAB = 1024
MAXT = 384
NODES = 131072
N_ROW = 16
N_COL = 8


def draw_tile_counts(key, part):
    key = jax.random.fold_in(key, 5)
    first, second = jax.random.split(key)
    counts = jax.random.randint(first, (N_ROW * N_COL,), MAXT // 4, MAXT + 1)
    chosen = jax.random.randint(second, (), 0, N_ROW * N_COL)
    counts = jnp.where(jnp.arange(N_ROW * N_COL) == chosen, MAXT, counts)
    return counts.reshape(N_ROW, N_COL).astype(jnp.int32)


def place_ends(entries, stream_key, low, largest):
    longest = entries.shape.index(max(entries.shape))
    spots = []
    for shift in (0, 1):
        where = [jax.random.randint(jax.random.fold_in(stream_key, axis), (), 0, length) for axis, length in enumerate(entries.shape)]
        where[longest] = (where[longest] + shift) % entries.shape[longest]
        spots.append(tuple(where))
    return entries.at[spots[0]].set(low).at[spots[1]].set(largest)


def shard_levels(key, dims, cuts, least, top_value):
    loudness = 1.0
    for axis_at, parts in cuts:
        draws = jax.random.uniform(jax.random.fold_in(jax.random.fold_in(key, 6), axis_at), (parts,), jnp.float32, least / len(cuts), top_value / len(cuts))
        loudness = loudness * jnp.repeat(jnp.exp(draws), dims[axis_at] // parts).reshape((-1,) + (1,) * (len(dims) - 1 - axis_at))
    return loudness


def gaussian(key, shape, spread, reach, pieces=(), kind=jnp.bfloat16):
    entries = spread * jax.random.normal(key, shape, jnp.float32)
    if pieces:
        entries = entries * shard_levels(key, shape, pieces, -0.22, 0.18)
    return jnp.clip(entries, -reach, reach).astype(kind)


def setup_inputs(seed: int = 0) -> dict:
    key_list = jax.random.split(jax.random.key(seed), 8)
    return {
        "tile_values": gaussian(key_list[0], (N_ROW, N_COL, MAXT, TILE, TILE), (MAXT * TILE * TILE // SLAB) ** -0.5, 0.078125, ((0, 16), (1, 8))),
        "tile_rows": place_ends(jax.random.randint(key_list[1], (N_ROW, N_COL, MAXT), 0, SLAB * N_COL // TILE), jax.random.fold_in(key_list[1], 1), 0, (SLAB * N_COL // TILE) - 1).astype(jnp.int32),
        "tile_cols": place_ends(jax.random.randint(key_list[2], (N_ROW, N_COL, MAXT), 0, SLAB * N_ROW // TILE), jax.random.fold_in(key_list[2], 1), 0, (SLAB * N_ROW // TILE) - 1).astype(jnp.int32),
        "tile_counts": draw_tile_counts(jax.random.fold_in(key_list[7], 71), 0),
        "out_grad": gaussian(key_list[4], (NODES, HIDDEN_SIZE), 1.0, 6.0, ((0, 128),)),
        "features": gaussian(key_list[5], (NODES, FEAT), 1.0, 6.0, ((0, 128),)),
        "weight": gaussian(key_list[6], (FEAT, HIDDEN_SIZE), HIDDEN_SIZE ** -0.5, 0.375),
    }


def reference(tile_values, tile_rows, tile_cols, tile_counts, out_grad, features, weight):
    groups = out_grad.reshape(N_ROW, N_COL * SLAB // TILE, TILE, HIDDEN_SIZE)
    total = jnp.zeros((N_ROW, N_COL, SLAB, HIDDEN_SIZE), jnp.float32)
    slots = jnp.arange(MAXT, dtype=jnp.int32)

    def one_device(carry, index):
        i = index // N_COL
        j = index % N_COL
        values = tile_values[i, j].astype(jnp.float32)
        rows_here = groups[i][tile_rows[i, j]].astype(jnp.float32)
        used = (slots < tile_counts[i, j]).astype(jnp.float32)
        prod = jnp.einsum('tab,tah->tbh', values, rows_here) * used[:, None, None]
        part = jnp.zeros((N_ROW * SLAB // TILE, TILE, HIDDEN_SIZE), jnp.float32).at[tile_cols[i, j]].add(prod)
        carry = carry.at[:, j].add(part.reshape(N_ROW, SLAB, HIDDEN_SIZE))
        return (carry, None)
    total, unused = lax.scan(one_device, total, jnp.arange(N_ROW * N_COL, dtype=jnp.int32))
    back = total.reshape(NODES, HIDDEN_SIZE)
    back_low = back.astype(jnp.bfloat16)
    feat_grad = jnp.dot(back_low, weight.T, preferred_element_type=jnp.float32).astype(jnp.bfloat16)
    weight_grad = jnp.dot(features.astype(jnp.float32).T, back, precision=lax.Precision.HIGHEST) / jnp.sqrt(jnp.float32(NODES))
    return (feat_grad, weight_grad)
```

```python
import functools

import jax
import jax.numpy as jnp
from jax import lax
from jax.experimental import pallas as pl
from jax.experimental.pallas import tpu as pltpu
from jax.sharding import PartitionSpec as P

MESH = pl.DeviceIdType.MESH
F32 = jnp.float32
BF16 = jnp.bfloat16
TILE = 128
NCOL = 8
NROW = 16
SLAB_TILES = 8
NH = 2
UNROLL = 16


def order_slots(rows_idx, cols_idx, count):
    slots = rows_idx.shape[0]
    col_tiles = NROW * SLAB_TILES
    pairs = (slots + col_tiles) // 2
    t = jnp.arange(slots, dtype=jnp.int32)
    c = jnp.arange(col_tiles, dtype=jnp.int32)
    used = t < count
    key = jnp.where(used, cols_idx, col_tiles)
    before = (key[:, None] == key[None, :]) & (t[None, :] < t[:, None])
    rank = jnp.sum(before.astype(jnp.int32), axis=1)
    hot = key[:, None] == c[None, :]
    number = jnp.sum(hot.astype(jnp.int32), axis=0)
    pair_number = (number + 1) // 2
    first = jnp.sum(jnp.where(c[None, :] < c[:, None], pair_number[None, :], 0), axis=1)
    place = 2 * jnp.sum(jnp.where(hot, first[None, :], 0), axis=1) + rank
    place = jnp.where(used, place, -1)
    q = jnp.arange(2 * pairs, dtype=jnp.int32)
    here = place[None, :] == q[:, None]
    vsrc = slots - jnp.sum(jnp.where(here, slots - t[None, :], 0), axis=1)
    rsrc = jnp.sum(jnp.where(here, rows_idx[None, :], 0), axis=1)
    p = jnp.arange(pairs, dtype=jnp.int32)
    starts = jnp.any((first[None, :] == p[:, None]) & (number[None, :] > 0), axis=1)
    keep = 1.0 - starts.astype(F32)
    last = jnp.where(number > 0, first + pair_number - 1, pairs)
    return vsrc.astype(jnp.int32), rsrc.astype(jnp.int32), keep, last.astype(jnp.int32)


def kernel(
    pairs, scale,
    vsrc, rsrc, keep, last, v_hbm, og_hbm, feat_hbm, w_hbm,
    fg_ref, wg_ref,
    v, og, feat, w, gt0, gt1, s, csend, crecv, q, r2, r1, f1, xr, bt, a_send, a_recv, b_buf, c_buf,
    local, ss, rs,
):
    gt = (gt0, gt1)
    wh = gt0.shape[1]
    slots = v_hbm.shape[0]
    row = lax.axis_index("row")
    col = lax.axis_index("col")
    xl, z, core = row // 8, lax.rem(row // 2, 4), lax.rem(row, 2)
    xh, y = col // 4, lax.rem(col, 4)

    def row_of(dx, dz, dc):
        a = 1 - xl if dx else xl
        b = 1 - core if dc else core
        return a * 8 + lax.rem(z + dz, 4) * 2 + b

    def col_of(dx, dy):
        a = 1 - xh if dx else xh
        return a * 4 + lax.rem(y + dy, 4)

    made = []

    def remote(src, dst, dev):
        i = len(made)
        copy = pltpu.make_async_remote_copy(
            src_ref=src, dst_ref=dst, send_sem=ss.at[i], recv_sem=rs.at[i], device_id=dev, device_id_type=MESH
        )
        made.append(copy)
        return copy

    load_og = pltpu.make_async_copy(og_hbm, og, local.at[0])
    load_v = pltpu.make_async_copy(v_hbm, v.at[pl.ds(0, slots)], local.at[1])
    load_f = pltpu.make_async_copy(feat_hbm, feat, local.at[2])
    load_w = pltpu.make_async_copy(w_hbm, w, local.at[3])
    load_og.start()
    barrier = pltpu.get_barrier_semaphore()
    for d in range(1, NCOL):
        pl.semaphore_signal(barrier, inc=1, device_id=(row, lax.rem(col + d, NCOL)), device_id_type=MESH)
    for d in range(1, NROW):
        pl.semaphore_signal(barrier, inc=1, device_id=(lax.rem(row + d, NROW), col), device_id_type=MESH)
    load_v.start()
    load_f.start()
    load_w.start()

    def turn(h):
        for k in range(SLAB_TILES):
            gt[h][col * SLAB_TILES + k] = og[k * TILE:(k + 1) * TILE, h * wh:(h + 1) * wh].T

    def block(h, dx, dy, half=None):
        at = col_of(dx, dy) * SLAB_TILES
        if half is None:
            return gt[h].at[pl.ds(at, SLAB_TILES)]
        return gt[h].at[pl.ds(at + half * (SLAB_TILES // 2), SLAB_TILES // 2)]

    gather = []
    for h in range(NH):
        m = {}
        m["x"] = remote(block(h, 0, 0), block(h, 0, 0), (row, col_of(1, 0)))
        for side in range(2):
            m["yp", side] = remote(block(h, side, 0), block(h, side, 0), (row, col_of(0, 1)))
            m["ym", side] = remote(block(h, side, 0), block(h, side, 0), (row, col_of(0, 3)))
            m["hp", side] = remote(block(h, side, 3, 0), block(h, side, 3, 0), (row, col_of(0, 1)))
            m["hm", side] = remote(block(h, side, 1, 1), block(h, side, 1, 1), (row, col_of(0, 3)))
        gather.append(m)

    def ag_start(h):
        for name in ("x", ("yp", 0), ("ym", 0)):
            gather[h][name].start()

    def ag_a(h):
        gather[h]["x"].wait_recv()
        gather[h]["yp", 1].start()
        gather[h]["ym", 1].start()

    def ag_b(h, side):
        gather[h]["yp", side].wait_recv()
        gather[h]["hp", side].start()
        gather[h]["ym", side].wait_recv()
        gather[h]["hm", side].start()

    def ag_d(h):
        for side in range(2):
            gather[h]["hp", side].wait_recv()
            gather[h]["hm", side].wait_recv()

    def compute(h, low, high, acc):
        def step(i, acc):
            for u in range(UNROLL):
                p = i * UNROLL + u
                g2 = jnp.concatenate([gt[h][rsrc[2 * p]], gt[h][rsrc[2 * p + 1]]], axis=1)
                v2 = jnp.concatenate([v[vsrc[2 * p]], v[vsrc[2 * p + 1]]], axis=0)
                acc = acc * keep[p] + jnp.dot(g2, v2, preferred_element_type=F32)
                s[p] = acc.astype(BF16)
            return acc

        return lax.fori_loop(low // UNROLL, high // UNROLL, step, acc)

    half_tiles = SLAB_TILES // 2
    order = [(1, 2), (0, 2), (1, 1), (1, 3), (0, 1), (0, 3), (1, 0), (0, 0)]
    reduce = []
    for h in range(NH):
        m = {}
        for dx, dz in order:
            m["c", dx, dz] = remote(csend.at[h, dx * 4 + dz], crecv.at[h, dx * 4 + dz], (row_of(0, 0, 1), col))
        for dx in range(2):
            for d, dz in enumerate((1, 3)):
                dev = (row_of(0, dz, 0), col)
                part = pl.ds(d * half_tiles, half_tiles)
                free = pl.ds((1 - d) * half_tiles, half_tiles)
                m["two", dx, d] = remote(q.at[h, dx * 4 + 2, part], r2.at[h, dx, d], dev)
                m["free", dx, d] = remote(q.at[h, dx * 4 + dz, free], r1.at[h, dx, d, free], dev)
                m["sum", dx, d] = remote(q.at[h, dx * 4 + dz, part], r1.at[h, dx, d, part], dev)
        m["x"] = remote(f1.at[h], xr.at[h], (row_of(1, 0, 0), col))
        reduce.append(m)

    def rs_send(h):
        for dx, dz in order:
            at = row_of(dx, dz, 1) * SLAB_TILES
            for k in range(SLAB_TILES):
                csend[h, dx * 4 + dz, k] = s[last[at + k]]
            reduce[h]["c", dx, dz].start()

    def rs_pair(h):
        for dx, dz in order:
            at = row_of(dx, dz, 0) * SLAB_TILES
            i = dx * 4 + dz
            reduce[h]["c", dx, dz].wait_recv()
            for k in range(SLAB_TILES):
                q[h, i, k] = (s[last[at + k]].astype(F32) + crecv[h, i, k].astype(F32)).astype(BF16)
            if dz == 2:
                reduce[h]["two", dx, 0].start()
                reduce[h]["two", dx, 1].start()
            elif dz == 1:
                reduce[h]["free", dx, 0].start()
            elif dz == 3:
                reduce[h]["free", dx, 1].start()

    def rs_relay(h, dx):
        for d, dz in enumerate((1, 3)):
            reduce[h]["two", dx, d].wait_recv()
            part = pl.ds(d * half_tiles, half_tiles)
            i = dx * 4 + dz
            q[h, i, part] = (q[h, i, part].astype(F32) + r2[h, dx, d].astype(F32)).astype(BF16)
            reduce[h]["sum", dx, d].start()

    def rs_landed(h, dx):
        for d in range(2):
            reduce[h]["free", dx, d].wait_recv()
            reduce[h]["sum", dx, d].wait_recv()

    def rs_cross(h):
        rs_landed(h, 1)
        f1[h] = (q[h, 4].astype(F32) + r1[h, 1, 0].astype(F32) + r1[h, 1, 1].astype(F32)).astype(BF16)
        reduce[h]["x"].start()

    def rs_end(h):
        rs_landed(h, 0)
        reduce[h]["x"].wait_recv()
        for k in range(SLAB_TILES):
            total = (
                q[h, 0, k].astype(F32) + r1[h, 0, 0, k].astype(F32) + r1[h, 0, 1, k].astype(F32) + xr[h, k].astype(F32)
            )
            bt[h * wh:(h + 1) * wh, k * TILE:(k + 1) * TILE] = total.astype(BF16)
        term = jnp.dot(bt[h * wh:(h + 1) * wh, :], feat[...], preferred_element_type=F32)
        chunk = a_send.shape[1]
        for k in range(wh // chunk):
            a_send[h * (wh // chunk) + k] = term[k * chunk:(k + 1) * chunk].astype(BF16)

    load_og.wait()
    turn(0)
    s[pairs] = jnp.zeros((wh, TILE), BF16)
    pl.semaphore_wait(barrier, NCOL + NROW - 2)
    ag_start(0)
    for h in range(1, NH):
        turn(h)
    v[slots] = jnp.zeros((TILE, TILE), BF16)
    ag_a(0)
    ag_b(0, 0)
    ag_start(1)
    ag_b(0, 1)
    ag_d(0)
    load_v.wait()
    load_f.wait()
    load_w.wait()
    half = pairs // 2
    acc = compute(0, 0, half, jnp.zeros((wh, TILE), F32))
    ag_a(1)
    ag_b(1, 0)
    compute(0, half, pairs, acc)
    rs_send(0)
    ag_b(1, 1)
    rs_pair(0)
    rs_relay(0, 1)
    rs_relay(0, 0)
    ag_d(1)
    acc = compute(1, 0, half, jnp.zeros((wh, TILE), F32))
    rs_cross(0)
    compute(1, half, pairs, acc)
    rs_send(1)
    rs_pair(1)
    rs_end(0)
    rs_relay(1, 1)
    rs_relay(1, 0)
    rs_cross(1)
    rs_end(1)

    stage_a = []
    for d in range(1, NCOL):
        to = lax.rem(col + d, NCOL)
        stage_a.append(remote(a_send.at[to], a_recv.at[d - 1], (row, to)))
        stage_a[-1].start()
    stage_b = []
    for d in range(1, NROW):
        stage_b.append(remote(b_buf.at[row], b_buf.at[row], (lax.rem(row + d, NROW), col)))
    stage_c = []
    for d in range(1, NCOL):
        stage_c.append(remote(c_buf.at[col], c_buf.at[col], (row, lax.rem(col + d, NCOL))))

    for k in range(SLAB_TILES):
        fg_ref[k * TILE:(k + 1) * TILE, :] = lax.dot_general(
            bt[:, k * TILE:(k + 1) * TILE], w[...], (((0,), (1,)), ((), ())), preferred_element_type=F32
        ).astype(BF16)

    total = a_send[col].astype(F32)
    for d in range(NCOL - 1):
        stage_a[d].wait_recv()
        total = total + a_recv[d].astype(F32)
    b_buf[row] = total.astype(BF16)
    for copy in stage_b:
        copy.start()
    for copy in stage_b:
        copy.wait_recv()
    total = b_buf[0].astype(F32)
    for i in range(1, NROW):
        total = total + b_buf[i].astype(F32)
    c_buf[col] = total * scale
    for copy in stage_c:
        copy.start()
    for copy in stage_c:
        copy.wait_recv()
    whole = jnp.concatenate([c_buf[i] for i in range(NCOL)], axis=0)
    wg_ref[...] = whole.T
    for copy in made:
        copy.wait_send()


def per_device(tile_values, tile_rows, tile_cols, tile_counts, out_grad, features, weight):
    values = tile_values[0, 0]
    slots = values.shape[0]
    slab, hidden = out_grad.shape
    width = features.shape[1]
    pairs = (slots + NROW * SLAB_TILES) // 2
    wh = hidden // NH
    scale = float(1.0 / (slab * NROW * NCOL) ** 0.5)
    vsrc, rsrc, keep, last = order_slots(tile_rows[0, 0], tile_cols[0, 0], tile_counts[0, 0])
    copies = NH * (9 + 8 + 12 + 1) + 2 * (NCOL - 1) + NROW - 1
    smem = pl.BlockSpec(memory_space=pltpu.SMEM)
    anyspace = pl.BlockSpec(memory_space=pl.ANY)
    vmem = pl.BlockSpec(memory_space=pltpu.VMEM)
    tiles = (SLAB_TILES, wh, TILE)
    half = (SLAB_TILES // 2, wh, TILE)
    return pl.pallas_call(
        functools.partial(kernel, pairs, scale),
        out_shape=(
            jax.ShapeDtypeStruct((slab, width), BF16),
            jax.ShapeDtypeStruct((width, hidden), F32),
        ),
        in_specs=[smem] * 4 + [anyspace] * 4,
        out_specs=(vmem, vmem),
        scratch_shapes=[
            pltpu.VMEM((slots + 1, TILE, TILE), BF16),
            pltpu.VMEM((slab, hidden), BF16),
            pltpu.VMEM((slab, width), BF16),
            pltpu.VMEM((width, hidden), BF16),
            pltpu.VMEM((NCOL * SLAB_TILES, wh, TILE), BF16),
            pltpu.VMEM((NCOL * SLAB_TILES, wh, TILE), BF16),
            pltpu.VMEM((pairs + 1, wh, TILE), BF16),
            pltpu.VMEM((NH, 8) + tiles, BF16),
            pltpu.VMEM((NH, 8) + tiles, BF16),
            pltpu.VMEM((NH, 8) + tiles, BF16),
            pltpu.VMEM((NH, 2, 2) + half, BF16),
            pltpu.VMEM((NH, 2, 2) + tiles, BF16),
            pltpu.VMEM((NH,) + tiles, BF16),
            pltpu.VMEM((NH,) + tiles, BF16),
            pltpu.VMEM((hidden, slab), BF16),
            pltpu.VMEM((NCOL, hidden // NCOL, width), BF16),
            pltpu.VMEM((NCOL - 1, hidden // NCOL, width), BF16),
            pltpu.VMEM((NROW, hidden // NCOL, width), BF16),
            pltpu.VMEM((NCOL, hidden // NCOL, width), F32),
            pltpu.SemaphoreType.DMA((4,)),
            pltpu.SemaphoreType.DMA((copies,)),
            pltpu.SemaphoreType.DMA((copies,)),
        ],
        compiler_params=pltpu.CompilerParams(
            collective_id=0, has_side_effects=True, vmem_limit_bytes=60 * 2**20
        ),
        cost_estimate=pl.CostEstimate(flops=2 * slots * TILE * TILE * hidden, bytes_accessed=16 * 2**20, transcendentals=0),
    )(vsrc, rsrc, keep, last, values, out_grad, features, weight)


def solution(mesh):
    placed = (
        P("row", "col", None, None, None),
        P("row", "col", None),
        P("row", "col", None),
        P("row", "col"),
        P(("row", "col"), None),
        P(("row", "col"), None),
        P(),
    )
    return jax.shard_map(
        per_device,
        mesh=mesh,
        in_specs=placed,
        out_specs=(P(("row", "col"), None), P()),
        check_vma=False,
    )
```

```python
import functools

import jax
import jax.numpy as jnp
from jax import lax
from jax.experimental import pallas as pl
from jax.experimental.pallas import tpu as pltpu
from jax.sharding import PartitionSpec as P

MESH = pl.DeviceIdType.MESH
F32 = jnp.float32
BF16 = jnp.bfloat16
TILE = 128
NCOL = 8
NROW = 16
SLAB_TILES = 8
NH = 2
UNROLL = 16
SEGMENTS = 4
BATCHES = 2


def turned(line, width):
    return jnp.broadcast_to(line, (width, line.shape[1])).T


def order_slots(rows, cols, count, pairs):
    slots = rows.shape[1]
    col_tiles = NROW * SLAB_TILES
    iota = lambda shape, axis: lax.broadcasted_iota(jnp.int32, shape, axis)
    pick = lambda mask, value, axis: jnp.sum(jnp.where(mask, value, 0), axis=axis, keepdims=True)
    t = iota((1, slots), 1)
    key = jnp.where(t < count, cols, col_tiles)
    t_down = iota((slots, TILE), 0)
    key_down = turned(key, TILE)
    rows_down = turned(rows, TILE)
    rank = jnp.zeros((slots, 1), jnp.int32)
    for k in range(0, slots, TILE):
        before = (key_down == key[:, k:k + TILE]) & (t[:, k:k + TILE] < t_down)
        rank = rank + pick(before, 1, 1)
    c = iota((1, col_tiles), 1)
    hot = key_down == c
    number = pick(hot, 1, 0)
    pair_number = (number + 1) >> 1
    lower = iota((col_tiles, col_tiles), 0) < c
    first = pick(lower, turned(pair_number, col_tiles), 0)
    place = 2 * pick(hot, first, 1) + rank
    place = jnp.where(t_down[:, :1] < count, place, -1)
    vsrc, rsrc = [], []
    for k in range(0, 2 * pairs, TILE):
        here = place == iota((1, TILE), 1) + k
        vsrc.append(slots - pick(here, slots - t_down, 0))
        rsrc.append(pick(here, rows_down, 0))
    first_down = turned(first, TILE)
    number_down = turned(number, TILE)
    keep = []
    for k in range(0, pairs, TILE):
        starts = (first_down == iota((1, TILE), 1) + k) & (number_down > 0)
        keep.append((1 - pick(starts, 1, 0)).astype(F32))
    last = jnp.where(number > 0, first + pair_number - 1, pairs)
    return vsrc, rsrc, keep, last


def kernel(
    pairs, scale,
    rows_ref, cols_ref, count_ref, v_hbm, og_hbm, feat_hbm, w_hbm,
    fg_ref, wg_ref,
    index_vm, keep_vm, index, keep, v, og, feat, w, *rest,
):
    gt = rest[:NH]
    s, csend, crecv, q, rx2, r2, r1, r0, f1, xr, bt, a_send, a_recv, b_buf, c_buf, local, ss, rs = rest[NH:]
    wh = gt[0].shape[1]
    slots = v_hbm.shape[2]
    batch_rows = NH * wh // BATCHES
    chunk = batch_rows // NCOL
    row = lax.axis_index("row")
    col = lax.axis_index("col")
    xl, z, core = row // 8, lax.rem(row // 2, 4), lax.rem(row, 2)
    xh, y = col // 4, lax.rem(col, 4)

    def row_of(dx, dz, dc):
        a = 1 - xl if dx else xl
        b = 1 - core if dc else core
        return a * 8 + lax.rem(z + dz, 4) * 2 + b

    def col_of(dx, dy):
        a = 1 - xh if dx else xh
        return a * 4 + lax.rem(y + dy, 4)

    made = []

    def remote(src, dst, dev):
        i = len(made)
        copy = pltpu.make_async_remote_copy(
            src_ref=src, dst_ref=dst, send_sem=ss.at[i], recv_sem=rs.at[i], device_id=dev, device_id_type=MESH
        )
        made.append(copy)
        return copy

    load_og = pltpu.make_async_copy(og_hbm, og, local.at[0])
    load_v = pltpu.make_async_copy(v_hbm.at[0, 0], v.at[pl.ds(0, slots)], local.at[1])
    load_f = pltpu.make_async_copy(feat_hbm, feat, local.at[2])
    load_w = pltpu.make_async_copy(w_hbm, w, local.at[3])
    load_og.start()
    barrier = pltpu.get_barrier_semaphore()
    for d in range(1, NCOL):
        pl.semaphore_signal(barrier, inc=1, device_id=(row, lax.rem(col + d, NCOL)), device_id_type=MESH)
    for d in range(1, NROW):
        pl.semaphore_signal(barrier, inc=1, device_id=(lax.rem(row + d, NROW), col), device_id_type=MESH)
    load_v.start()
    load_f.start()
    load_w.start()

    to_index = pltpu.make_async_copy(index_vm, index, local.at[4])
    to_keep = pltpu.make_async_copy(keep_vm, keep, local.at[5])

    def prepare():
        vsrc, rsrc, chain, last = order_slots(rows_ref[0], cols_ref[0], count_ref[0, 0], pairs)
        for k, line in enumerate(vsrc):
            index_vm[0:1, k * TILE:(k + 1) * TILE] = line
        for k, line in enumerate(rsrc):
            index_vm[1:2, k * TILE:(k + 1) * TILE] = line
        index_vm[2:3, 0:TILE] = last
        for k, line in enumerate(chain):
            keep_vm[0:1, k * TILE:(k + 1) * TILE] = line
        to_index.start()
        to_keep.start()
        v[slots] = jnp.zeros((TILE, TILE), BF16)
        s[pairs] = jnp.zeros((wh, TILE), BF16)

    def loaded():
        to_index.wait()
        to_keep.wait()
        load_v.wait()

    def turn(h):
        for k in range(SLAB_TILES):
            gt[h][col * SLAB_TILES + k] = og[k * TILE:(k + 1) * TILE, h * wh:(h + 1) * wh].T

    def block(h, dx, dy, half=None):
        at = col_of(dx, dy) * SLAB_TILES
        if half is None:
            return gt[h].at[pl.ds(at, SLAB_TILES)]
        return gt[h].at[pl.ds(at + half * (SLAB_TILES // 2), SLAB_TILES // 2)]

    gather = []
    for h in range(NH):
        m = {}
        yp, ym, xp = (row, col_of(0, 1)), (row, col_of(0, 3)), (row, col_of(1, 0))
        m["x1"] = remote(block(h, 0, 0), block(h, 0, 0), xp)
        m["x2"] = remote(block(h, 0, 2), block(h, 0, 2), xp)
        for side in range(2):
            m["yp", side] = remote(block(h, side, 0), block(h, side, 0), yp)
            m["ym", side] = remote(block(h, side, 0), block(h, side, 0), ym)
        m["hp"] = remote(block(h, 0, 3, 0), block(h, 0, 3, 0), yp)
        m["hm"] = remote(block(h, 0, 1, 1), block(h, 0, 1, 1), ym)
        gather.append(m)

    def ag_own(h):
        for name in (("yp", 0), ("ym", 0), "x1"):
            gather[h][name].start()

    def ag_half(h):
        gather[h]["yp", 0].wait_recv()
        gather[h]["hp"].start()
        gather[h]["ym", 0].wait_recv()
        gather[h]["hm"].start()

    def ag_side(h):
        gather[h]["x1"].wait_recv()
        gather[h]["yp", 1].start()
        gather[h]["ym", 1].start()

    def ag_cross(h):
        gather[h]["hp"].wait_recv()
        gather[h]["hm"].wait_recv()
        gather[h]["x2"].start()

    def ag_all(h):
        for name in (("yp", 1), ("ym", 1), "x2"):
            gather[h][name].wait_recv()

    chain = {}

    def compute(h, part):
        def step(i, acc):
            for u in range(UNROLL):
                p = i * UNROLL + u
                g2 = jnp.concatenate([gt[h][index[1, 2 * p]], gt[h][index[1, 2 * p + 1]]], axis=1)
                v2 = jnp.concatenate([v[index[0, 2 * p]], v[index[0, 2 * p + 1]]], axis=0)
                acc = acc * keep[0, p] + jnp.dot(g2, v2, preferred_element_type=F32)
                s[p] = acc.astype(BF16)
            return acc

        steps = pairs // UNROLL // SEGMENTS
        acc = chain[h] if part else jnp.zeros((wh, TILE), F32)
        chain[h] = lax.fori_loop(part * steps, (part + 1) * steps, step, acc)

    half_tiles = SLAB_TILES // 2
    order = [(1, 2), (1, 1), (1, 3), (0, 1), (0, 3), (0, 2), (1, 0), (0, 0)]
    reduce = []
    for h in range(NH):
        m = {}
        xp = (row_of(1, 0, 0), col)
        for dx, dz in order:
            m["c", dx, dz] = remote(csend.at[h, dx * 4 + dz], crecv.at[h, dx * 4 + dz], (row_of(0, 0, 1), col))
        m["x2"] = remote(q.at[h, 6], rx2.at[h], xp)
        for d, dz in enumerate((1, 3)):
            dev = (row_of(0, dz, 0), col)
            part = pl.ds(d * half_tiles, half_tiles)
            free = pl.ds((1 - d) * half_tiles, half_tiles)
            m["side", d] = remote(q.at[h, 4 + dz], r1.at[h, d], dev)
            m["two", d] = remote(q.at[h, 2, part], r2.at[h, d], dev)
            m["free", d] = remote(q.at[h, dz, free], r0.at[h, d, free], dev)
            m["sum", d] = remote(q.at[h, dz, part], r0.at[h, d, part], dev)
        m["x1"] = remote(f1.at[h], xr.at[h], xp)
        reduce.append(m)

    def rs_core(h):
        for dx, dz in order:
            at = row_of(dx, dz, 1) * SLAB_TILES
            for k in range(SLAB_TILES):
                csend[h, dx * 4 + dz, k] = s[index[2, at + k]]
            reduce[h]["c", dx, dz].start()

    def rs_pair(h):
        for dx, dz in order:
            at = row_of(dx, dz, 0) * SLAB_TILES
            i = dx * 4 + dz
            reduce[h]["c", dx, dz].wait_recv()
            for k in range(SLAB_TILES):
                q[h, i, k] = (s[index[2, at + k]].astype(F32) + crecv[h, i, k].astype(F32)).astype(BF16)
            if (dx, dz) == (1, 2):
                reduce[h]["x2"].start()
            elif dz in (1, 3):
                reduce[h]["side" if dx else "free", dz // 2].start()

    def rs_two(h):
        reduce[h]["x2"].wait_recv()
        for d in range(2):
            part = pl.ds(d * half_tiles, half_tiles)
            q[h, 2, part] = (q[h, 2, part].astype(F32) + rx2[h, part].astype(F32)).astype(BF16)
            reduce[h]["two", d].start()

    def rs_cross(h):
        reduce[h]["side", 0].wait_recv()
        reduce[h]["side", 1].wait_recv()
        f1[h] = (q[h, 4].astype(F32) + r1[h, 0].astype(F32) + r1[h, 1].astype(F32)).astype(BF16)
        reduce[h]["x1"].start()

    def rs_sum(h):
        for d, dz in enumerate((1, 3)):
            reduce[h]["two", d].wait_recv()
            part = pl.ds(d * half_tiles, half_tiles)
            q[h, dz, part] = (q[h, dz, part].astype(F32) + r2[h, d].astype(F32)).astype(BF16)
            reduce[h]["sum", d].start()

    def rs_end(h):
        reduce[h]["x1"].wait_recv()
        for d in range(2):
            reduce[h]["free", d].wait_recv()
            reduce[h]["sum", d].wait_recv()
        for k in range(SLAB_TILES):
            total = q[h, 0, k].astype(F32) + r0[h, 0, k].astype(F32) + r0[h, 1, k].astype(F32) + xr[h, k].astype(F32)
            bt[h * wh:(h + 1) * wh, k * TILE:(k + 1) * TILE] = total.astype(BF16)
        term = jnp.dot(bt[h * wh:(h + 1) * wh, :], feat[...], preferred_element_type=F32)
        for k in range(wh // chunk):
            at = h * (wh // chunk) + k
            a_send[at // NCOL, at % NCOL] = term[k * chunk:(k + 1) * chunk].astype(BF16)

    weight = []
    for b in range(BATCHES):
        first, second, third = [], [], []
        for d in range(1, NCOL):
            to = lax.rem(col + d, NCOL)
            first.append(remote(a_send.at[b, to], a_recv.at[b, d - 1], (row, to)))
            third.append(remote(c_buf.at[b, col], c_buf.at[b, col], (row, to)))
        for d in range(1, NROW):
            second.append(remote(b_buf.at[b, row], b_buf.at[b, row], (lax.rem(row + d, NROW), col)))
        weight.append((first, second, third))

    def wg_col(b):
        for copy in weight[b][0]:
            copy.start()

    def wg_row(b):
        total = a_send[b, col].astype(F32)
        for d in range(NCOL - 1):
            weight[b][0][d].wait_recv()
            total = total + a_recv[b, d].astype(F32)
        b_buf[b, row] = total.astype(BF16)
        for copy in weight[b][1]:
            copy.start()

    def wg_back(b):
        for copy in weight[b][1]:
            copy.wait_recv()
        total = b_buf[b, 0].astype(F32)
        for i in range(1, NROW):
            total = total + b_buf[b, i].astype(F32)
        c_buf[b, col] = total.astype(BF16)
        for copy in weight[b][2]:
            copy.start()

    def wg_end(b):
        for copy in weight[b][2]:
            copy.wait_recv()
        whole = jnp.concatenate([c_buf[b, i].astype(F32) for i in range(NCOL)], axis=0)
        wg_ref[:, b * batch_rows:(b + 1) * batch_rows] = whole.T * scale

    def feature():
        for k in range(SLAB_TILES):
            fg_ref[k * TILE:(k + 1) * TILE, :] = lax.dot_general(
                bt[:, k * TILE:(k + 1) * TILE], w[...], (((0,), (1,)), ((), ())), preferred_element_type=F32
            ).astype(BF16)

    load_og.wait()
    turn(0)
    pl.semaphore_wait(barrier, NCOL + NROW - 2)
    ag_own(0)
    turn(1)
    prepare()
    ag_half(0)
    ag_side(0)
    ag_cross(0)
    ag_own(1)
    ag_all(0)
    loaded()
    compute(0, 0)
    compute(0, 1)
    ag_half(1)
    ag_side(1)
    compute(0, 2)
    compute(0, 3)
    rs_core(0)
    ag_cross(1)
    rs_pair(0)
    ag_all(1)
    compute(1, 0)
    compute(1, 1)
    compute(1, 2)
    rs_two(0)
    rs_cross(0)
    compute(1, 3)
    rs_core(1)
    rs_sum(0)
    rs_pair(1)
    load_f.wait()
    load_w.wait()
    rs_end(0)
    wg_col(0)
    rs_two(1)
    rs_cross(1)
    wg_row(0)
    rs_sum(1)
    wg_back(0)
    rs_end(1)
    wg_col(1)
    feature()
    wg_row(1)
    wg_back(1)
    wg_end(0)
    wg_end(1)
    for copy in made:
        copy.wait_send()


def per_device(tile_values, tile_rows, tile_cols, tile_counts, out_grad, features, weight):
    slots = tile_values.shape[2]
    slab, hidden = out_grad.shape
    width = features.shape[1]
    pairs = (slots + NROW * SLAB_TILES) // 2
    wh = hidden // NH
    chunk = hidden // BATCHES // NCOL
    scale = float(1.0 / (slab * NROW * NCOL) ** 0.5)
    copies = NH * 26 + BATCHES * (2 * (NCOL - 1) + NROW - 1)
    smem = pl.BlockSpec(memory_space=pltpu.SMEM)
    anyspace = pl.BlockSpec(memory_space=pl.ANY)
    vmem = pl.BlockSpec(memory_space=pltpu.VMEM)
    tiles = (SLAB_TILES, wh, TILE)
    half = (SLAB_TILES // 2, wh, TILE)
    return pl.pallas_call(
        functools.partial(kernel, pairs, scale),
        out_shape=(
            jax.ShapeDtypeStruct((slab, width), BF16),
            jax.ShapeDtypeStruct((width, hidden), F32),
        ),
        in_specs=[vmem, vmem, smem] + [anyspace] * 4,
        out_specs=(vmem, vmem),
        scratch_shapes=[
            pltpu.VMEM((8, 2 * pairs), jnp.int32),
            pltpu.VMEM((8, pairs), F32),
            pltpu.SMEM((8, 2 * pairs), jnp.int32),
            pltpu.SMEM((8, pairs), F32),
            pltpu.VMEM((slots + 1, TILE, TILE), BF16),
            pltpu.VMEM((slab, hidden), BF16),
            pltpu.VMEM((slab, width), BF16),
            pltpu.VMEM((width, hidden), BF16),
        ]
        + [pltpu.VMEM((NCOL * SLAB_TILES, wh, TILE), BF16) for _ in range(NH)]
        + [
            pltpu.VMEM((pairs + 1, wh, TILE), BF16),
            pltpu.VMEM((NH, 8) + tiles, BF16),
            pltpu.VMEM((NH, 8) + tiles, BF16),
            pltpu.VMEM((NH, 8) + tiles, BF16),
            pltpu.VMEM((NH,) + tiles, BF16),
            pltpu.VMEM((NH, 2) + half, BF16),
            pltpu.VMEM((NH, 2) + tiles, BF16),
            pltpu.VMEM((NH, 2) + tiles, BF16),
            pltpu.VMEM((NH,) + tiles, BF16),
            pltpu.VMEM((NH,) + tiles, BF16),
            pltpu.VMEM((hidden, slab), BF16),
            pltpu.VMEM((BATCHES, NCOL, chunk, width), BF16),
            pltpu.VMEM((BATCHES, NCOL - 1, chunk, width), BF16),
            pltpu.VMEM((BATCHES, NROW, chunk, width), BF16),
            pltpu.VMEM((BATCHES, NCOL, chunk, width), BF16),
            pltpu.SemaphoreType.DMA((6,)),
            pltpu.SemaphoreType.DMA((copies,)),
            pltpu.SemaphoreType.DMA((copies,)),
        ],
        compiler_params=pltpu.CompilerParams(
            collective_id=0, has_side_effects=True, vmem_limit_bytes=60 * 2**20
        ),
        cost_estimate=pl.CostEstimate(flops=2 * slots * TILE * TILE * hidden, bytes_accessed=16 * 2**20, transcendentals=0),
    )(tile_rows, tile_cols, tile_counts, tile_values, out_grad, features, weight)


def solution(mesh):
    placed = (
        P("row", "col", None, None, None),
        P("row", "col", None),
        P("row", "col", None),
        P("row", "col"),
        P(("row", "col"), None),
        P(("row", "col"), None),
        P(),
    )
    return jax.shard_map(
        per_device,
        mesh=mesh,
        in_specs=placed,
        out_specs=(P(("row", "col"), None), P()),
        check_vma=False,
    )
```

```python
import functools

import jax
import jax.numpy as jnp
from jax import lax
from jax.experimental import pallas as pl
from jax.experimental.pallas import tpu as pltpu
from jax.sharding import PartitionSpec as P

MESH = pl.DeviceIdType.MESH
F32 = jnp.float32
BF16 = jnp.bfloat16
TILE = 128
NCOL = 8
NROW = 16
SLAB_TILES = 8
NH = 4
UNROLL = 32
SEGMENTS = 4
BATCHES = 2


def turned(line, width):
    return jnp.broadcast_to(line, (width, line.shape[1])).T


def order_slots(rows, cols, count, pairs):
    slots = rows.shape[1]
    col_tiles = NROW * SLAB_TILES
    iota = lambda shape, axis: lax.broadcasted_iota(jnp.int32, shape, axis)
    pick = lambda mask, value, axis: jnp.sum(jnp.where(mask, value, 0), axis=axis, keepdims=True)
    t = iota((1, slots), 1)
    key = jnp.where(t < count, cols, col_tiles)
    t_down = iota((slots, TILE), 0)
    key_down = turned(key, TILE)
    rows_down = turned(rows, TILE)
    rank = jnp.zeros((slots, 1), jnp.int32)
    for k in range(0, slots, TILE):
        before = (key_down == key[:, k:k + TILE]) & (t[:, k:k + TILE] < t_down)
        rank = rank + pick(before, 1, 1)
    c = iota((1, col_tiles), 1)
    hot = key_down == c
    number = pick(hot, 1, 0)
    pair_number = (number + 1) >> 1
    lower = iota((col_tiles, col_tiles), 0) < c
    first = pick(lower, turned(pair_number, col_tiles), 0)
    place = 2 * pick(hot, first, 1) + rank
    place = jnp.where(t_down[:, :1] < count, place, -1)
    vsrc, rsrc = [], []
    for k in range(0, 2 * pairs, TILE):
        here = place == iota((1, TILE), 1) + k
        vsrc.append(slots - pick(here, slots - t_down, 0))
        rsrc.append(pick(here, rows_down, 0))
    first_down = turned(first, TILE)
    number_down = turned(number, TILE)
    keep = []
    for k in range(0, pairs, TILE):
        starts = (first_down == iota((1, TILE), 1) + k) & (number_down > 0)
        keep.append((1 - pick(starts, 1, 0)).astype(F32))
    last = jnp.where(number > 0, first + pair_number - 1, pairs)
    return vsrc, rsrc, keep, last


def kernel(
    pairs, scale,
    rows_ref, cols_ref, count_ref, v_hbm, og_hbm, feat_hbm, w_hbm,
    fg_ref, wg_ref,
    index_vm, keep_vm, index, keep, v, og, feat, w, *rest,
):
    gt = rest[:NH]
    s, csend, crecv, q, rx2, r2, r1, r0, f1, xr, bt, a_send, a_recv, b_buf, c_buf, local, ss, rs = rest[NH:]
    wh = gt[0].shape[1]
    slots = v_hbm.shape[2]
    batch_rows = NH * wh // BATCHES
    chunk = batch_rows // NCOL
    row = lax.axis_index("row")
    col = lax.axis_index("col")
    xl, z, core = row // 8, lax.rem(row // 2, 4), lax.rem(row, 2)
    xh, y = col // 4, lax.rem(col, 4)

    def row_of(dx, dz, dc):
        a = 1 - xl if dx else xl
        b = 1 - core if dc else core
        return a * 8 + lax.rem(z + dz, 4) * 2 + b

    def col_of(dx, dy):
        a = 1 - xh if dx else xh
        return a * 4 + lax.rem(y + dy, 4)

    made = []

    def remote(src, dst, dev):
        i = len(made)
        copy = pltpu.make_async_remote_copy(
            src_ref=src, dst_ref=dst, send_sem=ss.at[i], recv_sem=rs.at[i], device_id=dev, device_id_type=MESH
        )
        made.append(copy)
        return copy

    load_og = pltpu.make_async_copy(og_hbm, og, local.at[0])
    load_v = pltpu.make_async_copy(v_hbm.at[0, 0], v.at[pl.ds(0, slots)], local.at[1])
    load_f = pltpu.make_async_copy(feat_hbm, feat, local.at[2])
    load_w = pltpu.make_async_copy(w_hbm, w, local.at[3])
    load_og.start()
    barrier = pltpu.get_barrier_semaphore()
    for d in range(1, NCOL):
        pl.semaphore_signal(barrier, inc=1, device_id=(row, lax.rem(col + d, NCOL)), device_id_type=MESH)
    for d in range(1, NROW):
        pl.semaphore_signal(barrier, inc=1, device_id=(lax.rem(row + d, NROW), col), device_id_type=MESH)
    load_v.start()
    load_f.start()
    load_w.start()

    to_index = pltpu.make_async_copy(index_vm, index, local.at[4])
    to_keep = pltpu.make_async_copy(keep_vm, keep, local.at[5])

    def prepare():
        vsrc, rsrc, chain, last = order_slots(rows_ref[0], cols_ref[0], count_ref[0, 0], pairs)
        for k, line in enumerate(vsrc):
            index_vm[0:1, k * TILE:(k + 1) * TILE] = line
        for k, line in enumerate(rsrc):
            index_vm[1:2, k * TILE:(k + 1) * TILE] = line
        index_vm[2:3, 0:TILE] = last
        for k, line in enumerate(chain):
            keep_vm[0:1, k * TILE:(k + 1) * TILE] = line
        to_index.start()
        to_keep.start()
        v[slots] = jnp.zeros((TILE, TILE), BF16)
        s[pairs] = jnp.zeros((wh, TILE), BF16)

    def loaded():
        to_index.wait()
        to_keep.wait()
        load_v.wait()

    def turn(h):
        for k in range(SLAB_TILES):
            gt[h][col * SLAB_TILES + k] = og[k * TILE:(k + 1) * TILE, h * wh:(h + 1) * wh].T

    def block(h, dx, dy, half=None):
        at = col_of(dx, dy) * SLAB_TILES
        if half is None:
            return gt[h].at[pl.ds(at, SLAB_TILES)]
        return gt[h].at[pl.ds(at + half * (SLAB_TILES // 2), SLAB_TILES // 2)]

    gather = []
    for h in range(NH):
        m = {}
        yp, ym, xp = (row, col_of(0, 1)), (row, col_of(0, 3)), (row, col_of(1, 0))
        m["x1"] = remote(block(h, 0, 0), block(h, 0, 0), xp)
        m["x2"] = remote(block(h, 0, 2), block(h, 0, 2), xp)
        for side in range(2):
            m["yp", side] = remote(block(h, side, 0), block(h, side, 0), yp)
            m["ym", side] = remote(block(h, side, 0), block(h, side, 0), ym)
        m["hp"] = remote(block(h, 0, 3, 0), block(h, 0, 3, 0), yp)
        m["hm"] = remote(block(h, 0, 1, 1), block(h, 0, 1, 1), ym)
        gather.append(m)

    def ag_own(h):
        for name in (("yp", 0), ("ym", 0), "x1"):
            gather[h][name].start()

    def ag_half(h):
        gather[h]["yp", 0].wait_recv()
        gather[h]["hp"].start()
        gather[h]["ym", 0].wait_recv()
        gather[h]["hm"].start()

    def ag_side(h):
        gather[h]["x1"].wait_recv()
        gather[h]["yp", 1].start()
        gather[h]["ym", 1].start()

    def ag_cross(h):
        gather[h]["hp"].wait_recv()
        gather[h]["hm"].wait_recv()
        gather[h]["x2"].start()

    def ag_all(h):
        for name in (("yp", 1), ("ym", 1), "x2"):
            gather[h][name].wait_recv()

    chain = {}

    def compute(h, part):
        def step(i, acc):
            for u in range(UNROLL):
                p = i * UNROLL + u
                g2 = jnp.concatenate([gt[h][index[1, 2 * p]], gt[h][index[1, 2 * p + 1]]], axis=1)
                v2 = jnp.concatenate([v[index[0, 2 * p]], v[index[0, 2 * p + 1]]], axis=0)
                acc = acc * keep[0, p] + jnp.dot(g2, v2, preferred_element_type=F32)
                s[p] = acc.astype(BF16)
            return acc

        steps = pairs // UNROLL // SEGMENTS
        acc = chain[h] if part else jnp.zeros((wh, TILE), F32)
        chain[h] = lax.fori_loop(part * steps, (part + 1) * steps, step, acc)

    half_tiles = SLAB_TILES // 2
    order = [(1, 2), (1, 1), (1, 3), (0, 1), (0, 3), (0, 2), (1, 0), (0, 0)]
    reduce = []
    for h in range(NH):
        m = {}
        xp = (row_of(1, 0, 0), col)
        for dx, dz in order:
            m["c", dx, dz] = remote(csend.at[h, dx * 4 + dz], crecv.at[h, dx * 4 + dz], (row_of(0, 0, 1), col))
        m["x2"] = remote(q.at[h, 6], rx2.at[h], xp)
        for d, dz in enumerate((1, 3)):
            dev = (row_of(0, dz, 0), col)
            part = pl.ds(d * half_tiles, half_tiles)
            free = pl.ds((1 - d) * half_tiles, half_tiles)
            m["side", d] = remote(q.at[h, 4 + dz], r1.at[h, d], dev)
            m["two", d] = remote(q.at[h, 2, part], r2.at[h, d], dev)
            m["free", d] = remote(q.at[h, dz, free], r0.at[h, d, free], dev)
            m["sum", d] = remote(q.at[h, dz, part], r0.at[h, d, part], dev)
        m["x1"] = remote(f1.at[h], xr.at[h], xp)
        reduce.append(m)

    def rs_core(h):
        for dx, dz in order:
            at = row_of(dx, dz, 1) * SLAB_TILES
            for k in range(SLAB_TILES):
                csend[h, dx * 4 + dz, k] = s[index[2, at + k]]
            reduce[h]["c", dx, dz].start()
        for dx, dz in order:
            at = row_of(dx, dz, 0) * SLAB_TILES
            for k in range(SLAB_TILES):
                q[h, dx * 4 + dz, k] = s[index[2, at + k]]

    def rs_pair(h):
        for dx, dz in order:
            i = dx * 4 + dz
            reduce[h]["c", dx, dz].wait_recv()
            q[h, i] = (q[h, i].astype(F32) + crecv[h, i].astype(F32)).astype(BF16)
            if (dx, dz) == (1, 2):
                reduce[h]["x2"].start()
            elif dz in (1, 3):
                reduce[h]["side" if dx else "free", dz // 2].start()

    def rs_two(h):
        reduce[h]["x2"].wait_recv()
        for d in range(2):
            part = pl.ds(d * half_tiles, half_tiles)
            q[h, 2, part] = (q[h, 2, part].astype(F32) + rx2[h, part].astype(F32)).astype(BF16)
            reduce[h]["two", d].start()

    def rs_cross(h):
        reduce[h]["side", 0].wait_recv()
        reduce[h]["side", 1].wait_recv()
        f1[h] = (q[h, 4].astype(F32) + r1[h, 0].astype(F32) + r1[h, 1].astype(F32)).astype(BF16)
        reduce[h]["x1"].start()

    def rs_sum(h):
        for d, dz in enumerate((1, 3)):
            reduce[h]["two", d].wait_recv()
            part = pl.ds(d * half_tiles, half_tiles)
            q[h, dz, part] = (q[h, dz, part].astype(F32) + r2[h, d].astype(F32)).astype(BF16)
            reduce[h]["sum", d].start()

    def rs_end(h):
        reduce[h]["x1"].wait_recv()
        for d in range(2):
            reduce[h]["free", d].wait_recv()
            reduce[h]["sum", d].wait_recv()
        for k in range(SLAB_TILES):
            total = q[h, 0, k].astype(F32) + r0[h, 0, k].astype(F32) + r0[h, 1, k].astype(F32) + xr[h, k].astype(F32)
            bt[h * wh:(h + 1) * wh, k * TILE:(k + 1) * TILE] = total.astype(BF16)
        term = jnp.dot(bt[h * wh:(h + 1) * wh, :], feat[...], preferred_element_type=F32)
        for k in range(wh // chunk):
            at = h * (wh // chunk) + k
            a_send[at // NCOL, at % NCOL] = term[k * chunk:(k + 1) * chunk].astype(BF16)

    weight = []
    for b in range(BATCHES):
        first, second, third = [], [], []
        for d in range(1, NCOL):
            to = lax.rem(col + d, NCOL)
            first.append(remote(a_send.at[b, to], a_recv.at[b, d - 1], (row, to)))
            third.append(remote(c_buf.at[b, col], c_buf.at[b, col], (row, to)))
        for d in range(1, NROW):
            second.append(remote(b_buf.at[b, row], b_buf.at[b, row], (lax.rem(row + d, NROW), col)))
        weight.append((first, second, third))

    def wg_col(b):
        for copy in weight[b][0]:
            copy.start()

    def wg_row(b):
        total = a_send[b, col].astype(F32)
        for d in range(NCOL - 1):
            weight[b][0][d].wait_recv()
            total = total + a_recv[b, d].astype(F32)
        b_buf[b, row] = total.astype(BF16)
        for copy in weight[b][1]:
            copy.start()

    def wg_back(b):
        for copy in weight[b][1]:
            copy.wait_recv()
        total = b_buf[b, 0].astype(F32)
        for i in range(1, NROW):
            total = total + b_buf[b, i].astype(F32)
        c_buf[b, col] = total.astype(BF16)
        for copy in weight[b][2]:
            copy.start()

    def wg_end(b):
        for copy in weight[b][2]:
            copy.wait_recv()
        whole = jnp.concatenate([c_buf[b, i].astype(F32) for i in range(NCOL)], axis=0)
        wg_ref[:, b * batch_rows:(b + 1) * batch_rows] = whole.T * scale

    def feature():
        for k in range(SLAB_TILES):
            fg_ref[k * TILE:(k + 1) * TILE, :] = lax.dot_general(
                bt[:, k * TILE:(k + 1) * TILE], w[...], (((0,), (1,)), ((), ())), preferred_element_type=F32
            ).astype(BF16)

    load_og.wait()
    turn(0)
    pl.semaphore_wait(barrier, NCOL + NROW - 2)
    ag_own(0)
    turn(1)
    ag_own(1)
    prepare()
    ag_half(0)
    ag_side(0)
    turn(2)
    ag_cross(0)
    turn(3)
    ag_half(1)
    ag_own(2)
    loaded()
    ag_cross(1)
    ag_side(1)
    ag_all(0)
    compute(0, 0)
    compute(0, 1)
    ag_half(2)
    compute(0, 2)
    ag_own(3)
    compute(0, 3)
    rs_core(0)
    ag_all(1)
    ag_side(2)
    compute(1, 0)
    ag_cross(2)
    compute(1, 1)
    compute(1, 2)
    ag_half(3)
    ag_side(3)
    rs_pair(0)
    compute(1, 3)
    rs_core(1)
    ag_all(2)
    compute(2, 0)
    ag_cross(3)
    compute(2, 1)
    rs_pair(1)
    compute(2, 2)
    compute(2, 3)
    rs_core(2)
    rs_two(0)
    rs_cross(0)
    ag_all(3)
    compute(3, 0)
    rs_pair(2)
    compute(3, 1)
    compute(3, 2)
    compute(3, 3)
    rs_two(1)
    rs_core(3)
    rs_cross(1)
    rs_sum(0)
    rs_two(2)
    rs_pair(3)
    rs_cross(2)
    rs_two(3)
    rs_cross(3)
    rs_sum(2)
    rs_sum(1)
    rs_sum(3)
    load_f.wait()
    load_w.wait()
    rs_end(2)
    rs_end(0)
    rs_end(1)
    wg_col(0)
    rs_end(3)
    wg_col(1)
    wg_row(0)
    wg_row(1)
    feature()
    wg_back(0)
    wg_back(1)
    wg_end(0)
    wg_end(1)
    for copy in made:
        copy.wait_send()


def per_device(tile_values, tile_rows, tile_cols, tile_counts, out_grad, features, weight):
    slots = tile_values.shape[2]
    slab, hidden = out_grad.shape
    width = features.shape[1]
    pairs = (slots + NROW * SLAB_TILES) // 2
    wh = hidden // NH
    chunk = hidden // BATCHES // NCOL
    scale = float(1.0 / (slab * NROW * NCOL) ** 0.5)
    copies = NH * 26 + BATCHES * (2 * (NCOL - 1) + NROW - 1)
    smem = pl.BlockSpec(memory_space=pltpu.SMEM)
    anyspace = pl.BlockSpec(memory_space=pl.ANY)
    vmem = pl.BlockSpec(memory_space=pltpu.VMEM)
    tiles = (SLAB_TILES, wh, TILE)
    half = (SLAB_TILES // 2, wh, TILE)
    return pl.pallas_call(
        functools.partial(kernel, pairs, scale),
        out_shape=(
            jax.ShapeDtypeStruct((slab, width), BF16),
            jax.ShapeDtypeStruct((width, hidden), F32),
        ),
        in_specs=[vmem, vmem, smem] + [anyspace] * 4,
        out_specs=(vmem, vmem),
        scratch_shapes=[
            pltpu.VMEM((8, 2 * pairs), jnp.int32),
            pltpu.VMEM((8, pairs), F32),
            pltpu.SMEM((8, 2 * pairs), jnp.int32),
            pltpu.SMEM((8, pairs), F32),
            pltpu.VMEM((slots + 1, TILE, TILE), BF16),
            pltpu.VMEM((slab, hidden), BF16),
            pltpu.VMEM((slab, width), BF16),
            pltpu.VMEM((width, hidden), BF16),
        ]
        + [pltpu.VMEM((NCOL * SLAB_TILES, wh, TILE), BF16) for _ in range(NH)]
        + [
            pltpu.VMEM((pairs + 1, wh, TILE), BF16),
            pltpu.VMEM((NH, 8) + tiles, BF16),
            pltpu.VMEM((NH, 8) + tiles, BF16),
            pltpu.VMEM((NH, 8) + tiles, BF16),
            pltpu.VMEM((NH,) + tiles, BF16),
            pltpu.VMEM((NH, 2) + half, BF16),
            pltpu.VMEM((NH, 2) + tiles, BF16),
            pltpu.VMEM((NH, 2) + tiles, BF16),
            pltpu.VMEM((NH,) + tiles, BF16),
            pltpu.VMEM((NH,) + tiles, BF16),
            pltpu.VMEM((hidden, slab), BF16),
            pltpu.VMEM((BATCHES, NCOL, chunk, width), BF16),
            pltpu.VMEM((BATCHES, NCOL - 1, chunk, width), BF16),
            pltpu.VMEM((BATCHES, NROW, chunk, width), BF16),
            pltpu.VMEM((BATCHES, NCOL, chunk, width), BF16),
            pltpu.SemaphoreType.DMA((6,)),
            pltpu.SemaphoreType.DMA((copies,)),
            pltpu.SemaphoreType.DMA((copies,)),
        ],
        compiler_params=pltpu.CompilerParams(
            collective_id=0, has_side_effects=True, vmem_limit_bytes=60 * 2**20
        ),
        cost_estimate=pl.CostEstimate(flops=2 * slots * TILE * TILE * hidden, bytes_accessed=16 * 2**20, transcendentals=0),
    )(tile_rows, tile_cols, tile_counts, tile_values, out_grad, features, weight)


def solution(mesh):
    placed = (
        P("row", "col", None, None, None),
        P("row", "col", None),
        P("row", "col", None),
        P("row", "col"),
        P(("row", "col"), None),
        P(("row", "col"), None),
        P(),
    )
    return jax.shard_map(
        per_device,
        mesh=mesh,
        in_specs=placed,
        out_specs=(P(("row", "col"), None), P()),
        check_vma=False,
    )
```

```python
import functools

import jax
import jax.numpy as jnp
from jax import lax
from jax.experimental import pallas as pl
from jax.experimental.pallas import tpu as pltpu
from jax.sharding import PartitionSpec as P

MESH = pl.DeviceIdType.MESH
F32 = jnp.float32
BF16 = jnp.bfloat16
TILE = 128
NCOL = 8
NROW = 16
SLAB_TILES = 8
NH = 4
UNROLL = 32
SEGMENTS = 4
BATCHES = 1


def turned(line, width):
    return jnp.broadcast_to(line, (width, line.shape[1])).T


def order_slots(rows, cols, count, pairs):
    slots = rows.shape[1]
    col_tiles = NROW * SLAB_TILES
    iota = lambda shape, axis: lax.broadcasted_iota(jnp.int32, shape, axis)
    pick = lambda mask, value, axis: jnp.sum(jnp.where(mask, value, 0), axis=axis, keepdims=True)
    t = iota((1, slots), 1)
    key = jnp.where(t < count, cols, col_tiles)
    t_down = iota((slots, TILE), 0)
    key_down = turned(key, TILE)
    rows_down = turned(rows, TILE)
    rank = jnp.zeros((slots, 1), jnp.int32)
    for k in range(0, slots, TILE):
        before = (key_down == key[:, k:k + TILE]) & (t[:, k:k + TILE] < t_down)
        rank = rank + pick(before, 1, 1)
    c = iota((1, col_tiles), 1)
    hot = key_down == c
    number = pick(hot, 1, 0)
    pair_number = (number + 1) >> 1
    lower = iota((col_tiles, col_tiles), 0) < c
    first = pick(lower, turned(pair_number, col_tiles), 0)
    place = 2 * pick(hot, first, 1) + rank
    place = jnp.where(t_down[:, :1] < count, place, -1)
    vsrc, rsrc = [], []
    for k in range(0, 2 * pairs, TILE):
        here = place == iota((1, TILE), 1) + k
        vsrc.append(slots - pick(here, slots - t_down, 0))
        rsrc.append(pick(here, rows_down, 0))
    first_down = turned(first, TILE)
    number_down = turned(number, TILE)
    keep = []
    for k in range(0, pairs, TILE):
        starts = (first_down == iota((1, TILE), 1) + k) & (number_down > 0)
        keep.append((1 - pick(starts, 1, 0)).astype(F32))
    last = jnp.where(number > 0, first + pair_number - 1, pairs)
    return vsrc, rsrc, keep, last


def kernel(
    pairs, scale,
    rows_ref, cols_ref, count_ref, v_hbm, og_hbm, feat_hbm, w_hbm,
    fg_ref, wg_ref,
    index_vm, keep_vm, index, keep, v, og, feat, w, *rest,
):
    gt = rest[:NH]
    s, csend, crecv, q, rx2, r2, r1, r0, f1, xr, bt, a_send, a_recv, b_buf, c_buf, local, ss, rs = rest[NH:]
    wh = gt[0].shape[1]
    slots = v_hbm.shape[2]
    batch_rows = NH * wh // BATCHES
    chunk = batch_rows // NROW
    row = lax.axis_index("row")
    col = lax.axis_index("col")
    xl, z, core = row // 8, lax.rem(row // 2, 4), lax.rem(row, 2)
    xh, y = col // 4, lax.rem(col, 4)

    def row_of(dx, dz, dc):
        a = 1 - xl if dx else xl
        b = 1 - core if dc else core
        return a * 8 + lax.rem(z + dz, 4) * 2 + b

    def col_of(dx, dy):
        a = 1 - xh if dx else xh
        return a * 4 + lax.rem(y + dy, 4)

    made = []

    def remote(src, dst, dev):
        i = len(made)
        copy = pltpu.make_async_remote_copy(
            src_ref=src, dst_ref=dst, send_sem=ss.at[i], recv_sem=rs.at[i], device_id=dev, device_id_type=MESH
        )
        made.append(copy)
        return copy

    load_og = pltpu.make_async_copy(og_hbm, og, local.at[0])
    load_v = pltpu.make_async_copy(v_hbm.at[0, 0], v.at[pl.ds(0, slots)], local.at[1])
    load_f = pltpu.make_async_copy(feat_hbm, feat, local.at[2])
    load_w = pltpu.make_async_copy(w_hbm, w, local.at[3])
    load_og.start()
    barrier = pltpu.get_barrier_semaphore()
    for d in range(1, NCOL):
        pl.semaphore_signal(barrier, inc=1, device_id=(row, lax.rem(col + d, NCOL)), device_id_type=MESH)
    for d in range(1, NROW):
        pl.semaphore_signal(barrier, inc=1, device_id=(lax.rem(row + d, NROW), col), device_id_type=MESH)
    load_v.start()
    load_f.start()
    load_w.start()

    to_index = pltpu.make_async_copy(index_vm, index, local.at[4])
    to_keep = pltpu.make_async_copy(keep_vm, keep, local.at[5])

    def prepare():
        vsrc, rsrc, chain, last = order_slots(rows_ref[0], cols_ref[0], count_ref[0, 0], pairs)
        for k, line in enumerate(vsrc):
            index_vm[0:1, k * TILE:(k + 1) * TILE] = line
        for k, line in enumerate(rsrc):
            index_vm[1:2, k * TILE:(k + 1) * TILE] = line
        index_vm[2:3, 0:TILE] = last
        for k, line in enumerate(chain):
            keep_vm[0:1, k * TILE:(k + 1) * TILE] = line
        to_index.start()
        to_keep.start()
        v[slots] = jnp.zeros((TILE, TILE), BF16)
        s[pairs] = jnp.zeros((wh, TILE), BF16)

    def loaded():
        to_index.wait()
        to_keep.wait()
        load_v.wait()

    def turn(h):
        for k in range(SLAB_TILES):
            gt[h][col * SLAB_TILES + k] = og[k * TILE:(k + 1) * TILE, h * wh:(h + 1) * wh].T

    def block(h, dx, dy, half=None):
        at = col_of(dx, dy) * SLAB_TILES
        if half is None:
            return gt[h].at[pl.ds(at, SLAB_TILES)]
        return gt[h].at[pl.ds(at + half * (SLAB_TILES // 2), SLAB_TILES // 2)]

    gather = []
    for h in range(NH):
        m = {}
        yp, ym, xp = (row, col_of(0, 1)), (row, col_of(0, 3)), (row, col_of(1, 0))
        m["x1"] = remote(block(h, 0, 0), block(h, 0, 0), xp)
        m["x2"] = remote(block(h, 0, 2), block(h, 0, 2), xp)
        for side in range(2):
            m["yp", side] = remote(block(h, side, 0), block(h, side, 0), yp)
            m["ym", side] = remote(block(h, side, 0), block(h, side, 0), ym)
        m["hp"] = remote(block(h, 0, 3, 0), block(h, 0, 3, 0), yp)
        m["hm"] = remote(block(h, 0, 1, 1), block(h, 0, 1, 1), ym)
        gather.append(m)

    def ag_own(h):
        for name in (("yp", 0), ("ym", 0), "x1"):
            gather[h][name].start()

    def ag_half(h):
        gather[h]["yp", 0].wait_recv()
        gather[h]["hp"].start()
        gather[h]["ym", 0].wait_recv()
        gather[h]["hm"].start()

    def ag_side(h):
        gather[h]["x1"].wait_recv()
        gather[h]["yp", 1].start()
        gather[h]["ym", 1].start()

    def ag_cross(h):
        gather[h]["hp"].wait_recv()
        gather[h]["hm"].wait_recv()
        gather[h]["x2"].start()

    def ag_all(h):
        for name in (("yp", 1), ("ym", 1), "x2"):
            gather[h][name].wait_recv()

    chain = {}

    def compute(h, part):
        def step(i, acc):
            for u in range(UNROLL):
                p = i * UNROLL + u
                g2 = jnp.concatenate([gt[h][index[1, 2 * p]], gt[h][index[1, 2 * p + 1]]], axis=1)
                v2 = jnp.concatenate([v[index[0, 2 * p]], v[index[0, 2 * p + 1]]], axis=0)
                acc = acc * keep[0, p] + jnp.dot(g2, v2, preferred_element_type=F32)
                s[p] = acc.astype(BF16)
            return acc

        steps = pairs // UNROLL // SEGMENTS
        acc = chain[h] if part else jnp.zeros((wh, TILE), F32)
        chain[h] = lax.fori_loop(part * steps, (part + 1) * steps, step, acc)

    half_tiles = SLAB_TILES // 2
    order = [(1, 2), (1, 1), (1, 3), (0, 1), (0, 3), (0, 2), (1, 0), (0, 0)]
    reduce = []
    for h in range(NH):
        m = {}
        xp = (row_of(1, 0, 0), col)
        for dx, dz in order:
            m["c", dx, dz] = remote(csend.at[h, dx * 4 + dz], crecv.at[h, dx * 4 + dz], (row_of(0, 0, 1), col))
        m["x2"] = remote(q.at[h, 6], rx2.at[h], xp)
        for d, dz in enumerate((1, 3)):
            dev = (row_of(0, dz, 0), col)
            part = pl.ds(d * half_tiles, half_tiles)
            free = pl.ds((1 - d) * half_tiles, half_tiles)
            m["side", d] = remote(q.at[h, 4 + dz], r1.at[h, d], dev)
            m["two", d] = remote(q.at[h, 2, part], r2.at[h, d], dev)
            m["free", d] = remote(q.at[h, dz, free], r0.at[h, d, free], dev)
            m["sum", d] = remote(q.at[h, dz, part], r0.at[h, d, part], dev)
        m["x1"] = remote(f1.at[h], xr.at[h], xp)
        reduce.append(m)

    def rs_core(h):
        for dx, dz in order:
            at = row_of(dx, dz, 1) * SLAB_TILES
            for k in range(SLAB_TILES):
                csend[h, dx * 4 + dz, k] = s[index[2, at + k]]
            reduce[h]["c", dx, dz].start()
        for dx, dz in order:
            at = row_of(dx, dz, 0) * SLAB_TILES
            for k in range(SLAB_TILES):
                q[h, dx * 4 + dz, k] = s[index[2, at + k]]

    def rs_pair(h):
        for dx, dz in order:
            i = dx * 4 + dz
            reduce[h]["c", dx, dz].wait_recv()
            q[h, i] = (q[h, i].astype(F32) + crecv[h, i].astype(F32)).astype(BF16)
            if (dx, dz) == (1, 2):
                reduce[h]["x2"].start()
            elif dz in (1, 3):
                reduce[h]["side" if dx else "free", dz // 2].start()

    def rs_two(h):
        reduce[h]["x2"].wait_recv()
        for d in range(2):
            part = pl.ds(d * half_tiles, half_tiles)
            q[h, 2, part] = (q[h, 2, part].astype(F32) + rx2[h, part].astype(F32)).astype(BF16)
            reduce[h]["two", d].start()

    def rs_cross(h):
        reduce[h]["side", 0].wait_recv()
        reduce[h]["side", 1].wait_recv()
        f1[h] = (q[h, 4].astype(F32) + r1[h, 0].astype(F32) + r1[h, 1].astype(F32)).astype(BF16)
        reduce[h]["x1"].start()

    def rs_sum(h):
        for d, dz in enumerate((1, 3)):
            reduce[h]["two", d].wait_recv()
            part = pl.ds(d * half_tiles, half_tiles)
            q[h, dz, part] = (q[h, dz, part].astype(F32) + r2[h, d].astype(F32)).astype(BF16)
            reduce[h]["sum", d].start()

    def rs_end(h):
        reduce[h]["x1"].wait_recv()
        for d in range(2):
            reduce[h]["free", d].wait_recv()
            reduce[h]["sum", d].wait_recv()
        for k in range(SLAB_TILES):
            total = q[h, 0, k].astype(F32) + r0[h, 0, k].astype(F32) + r0[h, 1, k].astype(F32) + xr[h, k].astype(F32)
            bt[h * wh:(h + 1) * wh, k * TILE:(k + 1) * TILE] = total.astype(BF16)

    before = len(made)
    weight = []
    for b in range(BATCHES):
        first, second, third = [], [], []
        for d in range(1, NROW):
            to = lax.rem(row + d, NROW)
            first.append(remote(a_send.at[b, to], a_recv.at[b, d - 1], (to, col)))
            third.append(remote(c_buf.at[b, row], c_buf.at[b, row], (to, col)))
        for d in range(1, NCOL):
            second.append(remote(b_buf.at[b, col], b_buf.at[b, col], (row, lax.rem(col + d, NCOL))))
        weight.append((first, second, third))

    def wg_term(low, high):
        term = jnp.dot(bt[low:high, :], feat[...], preferred_element_type=F32)
        for k in range(low // chunk, high // chunk):
            a_send[k // NROW, k % NROW] = term[k * chunk - low:(k + 1) * chunk - low].astype(BF16)

    def wg_col(b):
        for copy in weight[b][0]:
            copy.start()

    def wg_row(b):
        total = a_send[b, row].astype(F32)
        for d in range(NROW - 1):
            weight[b][0][d].wait_recv()
            total = total + a_recv[b, d].astype(F32)
        b_buf[b, col] = total.astype(BF16)
        for copy in weight[b][1]:
            copy.start()

    def wg_back(b):
        for copy in weight[b][1]:
            copy.wait_recv()
        total = b_buf[b, 0].astype(F32)
        for i in range(1, NCOL):
            total = total + b_buf[b, i].astype(F32)
        c_buf[b, row] = total.astype(BF16)
        for copy in weight[b][2]:
            copy.start()

    def wg_end(b):
        for copy in weight[b][2]:
            copy.wait_recv()
        whole = jnp.concatenate([c_buf[b, i].astype(F32) for i in range(NROW)], axis=0)
        wg_ref[:, b * batch_rows:(b + 1) * batch_rows] = whole.T * scale

    def feature():
        for k in range(SLAB_TILES):
            fg_ref[k * TILE:(k + 1) * TILE, :] = lax.dot_general(
                bt[:, k * TILE:(k + 1) * TILE], w[...], (((0,), (1,)), ((), ())), preferred_element_type=F32
            ).astype(BF16)

    load_og.wait()
    turn(0)
    pl.semaphore_wait(barrier, NCOL + NROW - 2)
    ag_own(0)
    turn(1)
    prepare()
    ag_own(1)
    ag_half(0)
    ag_side(0)
    ag_half(1)
    loaded()
    ag_cross(0)
    turn(2)
    ag_own(2)
    ag_side(1)
    ag_cross(1)
    ag_all(0)
    compute(0, 0)
    compute(0, 1)
    turn(3)
    ag_half(2)
    compute(0, 2)
    ag_own(3)
    compute(0, 3)
    ag_side(2)
    rs_core(0)
    ag_cross(2)
    ag_all(1)
    compute(1, 0)
    compute(1, 1)
    rs_pair(0)
    ag_half(3)
    compute(1, 2)
    compute(1, 3)
    ag_side(3)
    rs_core(1)
    ag_all(2)
    compute(2, 0)
    ag_cross(3)
    compute(2, 1)
    rs_two(0)
    compute(2, 2)
    rs_pair(1)
    compute(2, 3)
    rs_core(2)
    rs_sum(0)
    ag_all(3)
    compute(3, 0)
    compute(3, 1)
    rs_pair(2)
    compute(3, 2)
    rs_two(1)
    compute(3, 3)
    rs_cross(0)
    rs_core(3)
    rs_pair(3)
    rs_cross(2)
    rs_two(2)
    rs_cross(1)
    rs_two(3)
    rs_end(0)
    rs_sum(1)
    rs_cross(3)
    rs_sum(2)
    rs_sum(3)
    rs_end(2)
    rs_end(1)
    load_f.wait()
    load_w.wait()
    wg_term(0, (NH - 1) * wh)
    rs_end(3)
    wg_term((NH - 1) * wh, NH * wh)
    wg_col(0)
    feature()
    for copy in made[:before]:
        copy.wait_send()
    wg_row(0)
    wg_back(0)
    wg_end(0)
    for copy in made[before:]:
        copy.wait_send()


def per_device(tile_values, tile_rows, tile_cols, tile_counts, out_grad, features, weight):
    slots = tile_values.shape[2]
    slab, hidden = out_grad.shape
    width = features.shape[1]
    pairs = (slots + NROW * SLAB_TILES) // 2
    wh = hidden // NH
    chunk = hidden // BATCHES // NROW
    scale = float(1.0 / (slab * NROW * NCOL) ** 0.5)
    copies = NH * 26 + BATCHES * (2 * (NROW - 1) + NCOL - 1)
    smem = pl.BlockSpec(memory_space=pltpu.SMEM)
    anyspace = pl.BlockSpec(memory_space=pl.ANY)
    vmem = pl.BlockSpec(memory_space=pltpu.VMEM)
    tiles = (SLAB_TILES, wh, TILE)
    half = (SLAB_TILES // 2, wh, TILE)
    return pl.pallas_call(
        functools.partial(kernel, pairs, scale),
        out_shape=(
            jax.ShapeDtypeStruct((slab, width), BF16),
            jax.ShapeDtypeStruct((width, hidden), F32),
        ),
        in_specs=[vmem, vmem, smem] + [anyspace] * 4,
        out_specs=(vmem, vmem),
        scratch_shapes=[
            pltpu.VMEM((8, 2 * pairs), jnp.int32),
            pltpu.VMEM((8, pairs), F32),
            pltpu.SMEM((8, 2 * pairs), jnp.int32),
            pltpu.SMEM((8, pairs), F32),
            pltpu.VMEM((slots + 1, TILE, TILE), BF16),
            pltpu.VMEM((slab, hidden), BF16),
            pltpu.VMEM((slab, width), BF16),
            pltpu.VMEM((width, hidden), BF16),
        ]
        + [pltpu.VMEM((NCOL * SLAB_TILES, wh, TILE), BF16) for _ in range(NH)]
        + [
            pltpu.VMEM((pairs + 1, wh, TILE), BF16),
            pltpu.VMEM((NH, 8) + tiles, BF16),
            pltpu.VMEM((NH, 8) + tiles, BF16),
            pltpu.VMEM((NH, 8) + tiles, BF16),
            pltpu.VMEM((NH,) + tiles, BF16),
            pltpu.VMEM((NH, 2) + half, BF16),
            pltpu.VMEM((NH, 2) + tiles, BF16),
            pltpu.VMEM((NH, 2) + tiles, BF16),
            pltpu.VMEM((NH,) + tiles, BF16),
            pltpu.VMEM((NH,) + tiles, BF16),
            pltpu.VMEM((hidden, slab), BF16),
            pltpu.VMEM((BATCHES, NROW, chunk, width), BF16),
            pltpu.VMEM((BATCHES, NROW - 1, chunk, width), BF16),
            pltpu.VMEM((BATCHES, NCOL, chunk, width), BF16),
            pltpu.VMEM((BATCHES, NROW, chunk, width), BF16),
            pltpu.SemaphoreType.DMA((6,)),
            pltpu.SemaphoreType.DMA((copies,)),
            pltpu.SemaphoreType.DMA((copies,)),
        ],
        compiler_params=pltpu.CompilerParams(
            collective_id=0, has_side_effects=True, vmem_limit_bytes=60 * 2**20
        ),
        cost_estimate=pl.CostEstimate(flops=2 * slots * TILE * TILE * hidden, bytes_accessed=16 * 2**20, transcendentals=0),
    )(tile_rows, tile_cols, tile_counts, tile_values, out_grad, features, weight)


def solution(mesh):
    placed = (
        P("row", "col", None, None, None),
        P("row", "col", None),
        P("row", "col", None),
        P("row", "col"),
        P(("row", "col"), None),
        P(("row", "col"), None),
        P(),
    )
    return jax.shard_map(
        per_device,
        mesh=mesh,
        in_specs=placed,
        out_specs=(P(("row", "col"), None), P()),
        check_vma=False,
    )
```

```python
import functools

import jax
import jax.numpy as jnp
from jax import lax
from jax.experimental import pallas as pl
from jax.experimental.pallas import tpu as pltpu
from jax.sharding import PartitionSpec as P

MESH = pl.DeviceIdType.MESH
F32 = jnp.float32
BF16 = jnp.bfloat16
TILE = 128
NCOL = 8
NROW = 16
SLAB_TILES = 8
NH = 4
UNROLL = 32
SEGMENTS = 4
BATCHES = 1


def turned(line, width):
    return jnp.broadcast_to(line, (width, line.shape[1])).T


def order_slots(rows, cols, count, pairs):
    slots = rows.shape[1]
    col_tiles = NROW * SLAB_TILES
    iota = lambda shape, axis: lax.broadcasted_iota(jnp.int32, shape, axis)
    pick = lambda mask, value, axis: jnp.sum(jnp.where(mask, value, 0), axis=axis, keepdims=True)
    t = iota((1, slots), 1)
    key = jnp.where(t < count, cols, col_tiles)
    t_down = iota((slots, TILE), 0)
    key_down = turned(key, TILE)
    rows_down = turned(rows, TILE)
    rank = jnp.zeros((slots, 1), jnp.int32)
    for k in range(0, slots, TILE):
        before = (key_down == key[:, k:k + TILE]) & (t[:, k:k + TILE] < t_down)
        rank = rank + pick(before, 1, 1)
    c = iota((1, col_tiles), 1)
    hot = key_down == c
    number = pick(hot, 1, 0)
    pair_number = (number + 1) >> 1
    lower = iota((col_tiles, col_tiles), 0) < c
    first = pick(lower, turned(pair_number, col_tiles), 0)
    place = 2 * pick(hot, first, 1) + rank
    place = jnp.where(t_down[:, :1] < count, place, -1)
    vsrc, rsrc = [], []
    for k in range(0, 2 * pairs, TILE):
        here = place == iota((1, TILE), 1) + k
        vsrc.append(slots - pick(here, slots - t_down, 0))
        rsrc.append(pick(here, rows_down, 0))
    first_down = turned(first, TILE)
    number_down = turned(number, TILE)
    keep = []
    for k in range(0, pairs, TILE):
        starts = (first_down == iota((1, TILE), 1) + k) & (number_down > 0)
        keep.append((1 - pick(starts, 1, 0)).astype(F32))
    last = jnp.where(number > 0, first + pair_number - 1, pairs)
    return vsrc, rsrc, keep, last


def kernel(
    pairs, scale,
    rows_ref, cols_ref, count_ref, v_hbm, og_hbm, feat_hbm, w_hbm,
    fg_ref, wg_ref,
    index_vm, keep_vm, index, keep, v, og, feat, w, *rest,
):
    gt = rest[:NH]
    s, csend, crecv, q, rx2, r2, r1, r0, f1, xr, bt, a_send, a_recv, b_buf, c_buf, local, ss, rs = rest[NH:]
    wh = gt[0].shape[1]
    slots = v_hbm.shape[2]
    batch_rows = NH * wh // BATCHES
    chunk = batch_rows // NROW
    row = lax.axis_index("row")
    col = lax.axis_index("col")
    xl, z, core = row // 8, lax.rem(row // 2, 4), lax.rem(row, 2)
    xh, y = col // 4, lax.rem(col, 4)

    def row_of(dx, dz, dc):
        a = 1 - xl if dx else xl
        b = 1 - core if dc else core
        return a * 8 + lax.rem(z + dz, 4) * 2 + b

    def col_of(dx, dy):
        a = 1 - xh if dx else xh
        return a * 4 + lax.rem(y + dy, 4)

    made = []

    def remote(src, dst, dev):
        i = len(made)
        copy = pltpu.make_async_remote_copy(
            src_ref=src, dst_ref=dst, send_sem=ss.at[i], recv_sem=rs.at[i], device_id=dev, device_id_type=MESH
        )
        made.append(copy)
        return copy

    load_og = pltpu.make_async_copy(og_hbm, og, local.at[0])
    load_v = pltpu.make_async_copy(v_hbm.at[0, 0], v.at[pl.ds(0, slots)], local.at[1])
    load_f = pltpu.make_async_copy(feat_hbm, feat, local.at[2])
    load_w = pltpu.make_async_copy(w_hbm, w, local.at[3])
    load_og.start()
    barrier = pltpu.get_barrier_semaphore()
    for d in range(1, NCOL):
        pl.semaphore_signal(barrier, inc=1, device_id=(row, lax.rem(col + d, NCOL)), device_id_type=MESH)
    for d in range(1, NROW):
        pl.semaphore_signal(barrier, inc=1, device_id=(lax.rem(row + d, NROW), col), device_id_type=MESH)
    load_v.start()
    load_f.start()
    load_w.start()

    to_index = pltpu.make_async_copy(index_vm, index, local.at[4])
    to_keep = pltpu.make_async_copy(keep_vm, keep, local.at[5])

    def prepare():
        vsrc, rsrc, chain, last = order_slots(rows_ref[0], cols_ref[0], count_ref[0, 0], pairs)
        for k, line in enumerate(vsrc):
            index_vm[0:1, k * TILE:(k + 1) * TILE] = line
        for k, line in enumerate(rsrc):
            index_vm[1:2, k * TILE:(k + 1) * TILE] = line
        index_vm[2:3, 0:TILE] = last
        for k, line in enumerate(chain):
            keep_vm[0:1, k * TILE:(k + 1) * TILE] = line
        to_index.start()
        to_keep.start()
        v[slots] = jnp.zeros((TILE, TILE), BF16)
        s[pairs] = jnp.zeros((wh, TILE), BF16)

    def loaded():
        to_index.wait()
        to_keep.wait()
        load_v.wait()

    def turn(h):
        for k in range(SLAB_TILES):
            gt[h][col * SLAB_TILES + k] = og[k * TILE:(k + 1) * TILE, h * wh:(h + 1) * wh].T

    def block(h, dx, dy, half=None):
        at = col_of(dx, dy) * SLAB_TILES
        if half is None:
            return gt[h].at[pl.ds(at, SLAB_TILES)]
        return gt[h].at[pl.ds(at + half * (SLAB_TILES // 2), SLAB_TILES // 2)]

    gather = []
    for h in range(NH):
        m = {}
        yp, ym, xp = (row, col_of(0, 1)), (row, col_of(0, 3)), (row, col_of(1, 0))
        m["x1"] = remote(block(h, 0, 0), block(h, 0, 0), xp)
        m["x2"] = remote(block(h, 0, 2), block(h, 0, 2), xp)
        for side in range(2):
            m["yp", side] = remote(block(h, side, 0), block(h, side, 0), yp)
            m["ym", side] = remote(block(h, side, 0), block(h, side, 0), ym)
        m["hp"] = remote(block(h, 0, 3, 0), block(h, 0, 3, 0), yp)
        m["hm"] = remote(block(h, 0, 1, 1), block(h, 0, 1, 1), ym)
        gather.append(m)

    def ag_own(h):
        for name in (("yp", 0), ("ym", 0), "x1"):
            gather[h][name].start()

    def ag_half(h):
        gather[h]["yp", 0].wait_recv()
        gather[h]["hp"].start()
        gather[h]["ym", 0].wait_recv()
        gather[h]["hm"].start()

    def ag_side(h):
        gather[h]["x1"].wait_recv()
        gather[h]["yp", 1].start()
        gather[h]["ym", 1].start()

    def ag_cross(h):
        gather[h]["hp"].wait_recv()
        gather[h]["hm"].wait_recv()
        gather[h]["x2"].start()

    def ag_all(h):
        for name in (("yp", 1), ("ym", 1), "x2"):
            gather[h][name].wait_recv()

    chain = {}

    def compute(h, part):
        def step(i, acc):
            for u in range(UNROLL):
                p = i * UNROLL + u
                g2 = jnp.concatenate([gt[h][index[1, 2 * p]], gt[h][index[1, 2 * p + 1]]], axis=1)
                v2 = jnp.concatenate([v[index[0, 2 * p]], v[index[0, 2 * p + 1]]], axis=0)
                acc = acc * keep[0, p] + jnp.dot(g2, v2, preferred_element_type=F32)
                s[p] = acc.astype(BF16)
            return acc

        steps = pairs // UNROLL // SEGMENTS
        acc = chain[h] if part else jnp.zeros((wh, TILE), F32)
        chain[h] = lax.fori_loop(part * steps, (part + 1) * steps, step, acc)

    half_tiles = SLAB_TILES // 2
    order = [(1, 2), (1, 1), (1, 3), (0, 1), (0, 3), (0, 2), (1, 0), (0, 0)]
    reduce = []
    for h in range(NH):
        m = {}
        xp = (row_of(1, 0, 0), col)
        for dx, dz in order:
            m["c", dx, dz] = remote(csend.at[h, dx * 4 + dz], crecv.at[h, dx * 4 + dz], (row_of(0, 0, 1), col))
        m["x2"] = remote(q.at[h, 6], rx2.at[h], xp)
        for d, dz in enumerate((1, 3)):
            dev = (row_of(0, dz, 0), col)
            part = pl.ds(d * half_tiles, half_tiles)
            free = pl.ds((1 - d) * half_tiles, half_tiles)
            m["side", d] = remote(q.at[h, 4 + dz], r1.at[h, d], dev)
            m["two", d] = remote(q.at[h, 2, part], r2.at[h, d], dev)
            m["free", d] = remote(q.at[h, dz, free], r0.at[h, d, free], dev)
            m["sum", d] = remote(q.at[h, dz, part], r0.at[h, d, part], dev)
        m["x1"] = remote(f1.at[h], xr.at[h], xp)
        reduce.append(m)

    def rs_core(h):
        for dx, dz in order:
            at = row_of(dx, dz, 1) * SLAB_TILES
            for k in range(SLAB_TILES):
                csend[h, dx * 4 + dz, k] = s[index[2, at + k]]
            reduce[h]["c", dx, dz].start()
        for dx, dz in order:
            at = row_of(dx, dz, 0) * SLAB_TILES
            for k in range(SLAB_TILES):
                q[h, dx * 4 + dz, k] = s[index[2, at + k]]

    def rs_pair(h):
        for dx, dz in order:
            i = dx * 4 + dz
            reduce[h]["c", dx, dz].wait_recv()
            q[h, i] = (q[h, i].astype(F32) + crecv[h, i].astype(F32)).astype(BF16)
            if (dx, dz) == (1, 2):
                reduce[h]["x2"].start()
            elif dz in (1, 3):
                reduce[h]["side" if dx else "free", dz // 2].start()

    def rs_two(h):
        reduce[h]["x2"].wait_recv()
        for d in range(2):
            part = pl.ds(d * half_tiles, half_tiles)
            q[h, 2, part] = (q[h, 2, part].astype(F32) + rx2[h, part].astype(F32)).astype(BF16)
            reduce[h]["two", d].start()

    def rs_cross(h):
        reduce[h]["side", 0].wait_recv()
        reduce[h]["side", 1].wait_recv()
        f1[h] = (q[h, 4].astype(F32) + r1[h, 0].astype(F32) + r1[h, 1].astype(F32)).astype(BF16)
        reduce[h]["x1"].start()

    def rs_sum(h):
        for d, dz in enumerate((1, 3)):
            reduce[h]["two", d].wait_recv()
            part = pl.ds(d * half_tiles, half_tiles)
            q[h, dz, part] = (q[h, dz, part].astype(F32) + r2[h, d].astype(F32)).astype(BF16)
            reduce[h]["sum", d].start()

    def rs_end(h):
        reduce[h]["x1"].wait_recv()
        for d in range(2):
            reduce[h]["free", d].wait_recv()
            reduce[h]["sum", d].wait_recv()
        for k in range(SLAB_TILES):
            total = q[h, 0, k].astype(F32) + r0[h, 0, k].astype(F32) + r0[h, 1, k].astype(F32) + xr[h, k].astype(F32)
            bt[h * wh:(h + 1) * wh, k * TILE:(k + 1) * TILE] = total.astype(BF16)

    before = len(made)
    weight = []
    for b in range(BATCHES):
        first, second, third = [], [], []
        for k, (dx, dz, dc) in enumerate(
            (dx, dz, dc) for dx in (1, 0) for dz in (2, 1, 3, 0) for dc in (1, 0) if dx or dz or dc
        ):
            to = row_of(dx, dz, dc)
            first.append(remote(a_send.at[b, to], a_recv.at[b, k], (to, col)))
            third.append(remote(c_buf.at[b, row], c_buf.at[b, row], (to, col)))
        for dx, dy in ((1, 2), (1, 1), (1, 3), (1, 0), (0, 2), (0, 1), (0, 3)):
            second.append(remote(b_buf.at[b, col], b_buf.at[b, col], (row, col_of(dx, dy))))
        weight.append((first, second, third))

    def wg_term(low, high):
        term = jnp.dot(bt[low:high, :], feat[...], preferred_element_type=F32)
        for k in range(low // chunk, high // chunk):
            a_send[k // NROW, k % NROW] = term[k * chunk - low:(k + 1) * chunk - low].astype(BF16)

    def wg_col(b):
        for copy in weight[b][0]:
            copy.start()

    def wg_row(b):
        total = a_send[b, row].astype(F32)
        for d in range(NROW - 1):
            weight[b][0][d].wait_recv()
            total = total + a_recv[b, d].astype(F32)
        b_buf[b, col] = total.astype(BF16)
        for copy in weight[b][1]:
            copy.start()

    def wg_back(b):
        for copy in weight[b][1]:
            copy.wait_recv()
        total = b_buf[b, 0].astype(F32)
        for i in range(1, NCOL):
            total = total + b_buf[b, i].astype(F32)
        c_buf[b, row] = total.astype(BF16)
        for copy in weight[b][2]:
            copy.start()

    def wg_end(b):
        for copy in weight[b][2]:
            copy.wait_recv()
        whole = jnp.concatenate([c_buf[b, i].astype(F32) for i in range(NROW)], axis=0)
        wg_ref[:, b * batch_rows:(b + 1) * batch_rows] = whole.T * scale

    def feature():
        for k in range(SLAB_TILES):
            fg_ref[k * TILE:(k + 1) * TILE, :] = lax.dot_general(
                bt[:, k * TILE:(k + 1) * TILE], w[...], (((0,), (1,)), ((), ())), preferred_element_type=F32
            ).astype(BF16)

    load_og.wait()
    turn(0)
    pl.semaphore_wait(barrier, NCOL + NROW - 2)
    ag_own(0)
    turn(1)
    prepare()
    ag_own(1)
    ag_half(0)
    ag_side(0)
    ag_half(1)
    loaded()
    ag_cross(0)
    turn(2)
    ag_own(2)
    ag_side(1)
    ag_cross(1)
    ag_all(0)
    compute(0, 0)
    compute(0, 1)
    turn(3)
    ag_half(2)
    compute(0, 2)
    ag_own(3)
    compute(0, 3)
    ag_side(2)
    rs_core(0)
    ag_cross(2)
    ag_all(1)
    compute(1, 0)
    compute(1, 1)
    rs_pair(0)
    ag_half(3)
    compute(1, 2)
    compute(1, 3)
    ag_side(3)
    rs_core(1)
    ag_all(2)
    compute(2, 0)
    ag_cross(3)
    compute(2, 1)
    rs_two(0)
    compute(2, 2)
    rs_pair(1)
    compute(2, 3)
    rs_core(2)
    rs_sum(0)
    ag_all(3)
    compute(3, 0)
    compute(3, 1)
    rs_pair(2)
    compute(3, 2)
    rs_two(1)
    compute(3, 3)
    rs_cross(0)
    rs_core(3)
    rs_pair(3)
    rs_cross(2)
    rs_two(2)
    rs_cross(1)
    rs_two(3)
    rs_end(0)
    rs_sum(1)
    rs_cross(3)
    rs_sum(2)
    rs_sum(3)
    rs_end(2)
    rs_end(1)
    load_f.wait()
    load_w.wait()
    wg_term(0, (NH - 1) * wh)
    rs_end(3)
    wg_term((NH - 1) * wh, NH * wh)
    wg_col(0)
    feature()
    for copy in made[:before]:
        copy.wait_send()
    wg_row(0)
    wg_back(0)
    wg_end(0)
    for copy in made[before:]:
        copy.wait_send()


def per_device(tile_values, tile_rows, tile_cols, tile_counts, out_grad, features, weight):
    slots = tile_values.shape[2]
    slab, hidden = out_grad.shape
    width = features.shape[1]
    pairs = (slots + NROW * SLAB_TILES) // 2
    wh = hidden // NH
    chunk = hidden // BATCHES // NROW
    scale = float(1.0 / (slab * NROW * NCOL) ** 0.5)
    copies = NH * 26 + BATCHES * (2 * (NROW - 1) + NCOL - 1)
    smem = pl.BlockSpec(memory_space=pltpu.SMEM)
    anyspace = pl.BlockSpec(memory_space=pl.ANY)
    vmem = pl.BlockSpec(memory_space=pltpu.VMEM)
    tiles = (SLAB_TILES, wh, TILE)
    half = (SLAB_TILES // 2, wh, TILE)
    return pl.pallas_call(
        functools.partial(kernel, pairs, scale),
        out_shape=(
            jax.ShapeDtypeStruct((slab, width), BF16),
            jax.ShapeDtypeStruct((width, hidden), F32),
        ),
        in_specs=[vmem, vmem, smem] + [anyspace] * 4,
        out_specs=(vmem, vmem),
        scratch_shapes=[
            pltpu.VMEM((8, 2 * pairs), jnp.int32),
            pltpu.VMEM((8, pairs), F32),
            pltpu.SMEM((8, 2 * pairs), jnp.int32),
            pltpu.SMEM((8, pairs), F32),
            pltpu.VMEM((slots + 1, TILE, TILE), BF16),
            pltpu.VMEM((slab, hidden), BF16),
            pltpu.VMEM((slab, width), BF16),
            pltpu.VMEM((width, hidden), BF16),
        ]
        + [pltpu.VMEM((NCOL * SLAB_TILES, wh, TILE), BF16) for _ in range(NH)]
        + [
            pltpu.VMEM((pairs + 1, wh, TILE), BF16),
            pltpu.VMEM((NH, 8) + tiles, BF16),
            pltpu.VMEM((NH, 8) + tiles, BF16),
            pltpu.VMEM((NH, 8) + tiles, BF16),
            pltpu.VMEM((NH,) + tiles, BF16),
            pltpu.VMEM((NH, 2) + half, BF16),
            pltpu.VMEM((NH, 2) + tiles, BF16),
            pltpu.VMEM((NH, 2) + tiles, BF16),
            pltpu.VMEM((NH,) + tiles, BF16),
            pltpu.VMEM((NH,) + tiles, BF16),
            pltpu.VMEM((hidden, slab), BF16),
            pltpu.VMEM((BATCHES, NROW, chunk, width), BF16),
            pltpu.VMEM((BATCHES, NROW - 1, chunk, width), BF16),
            pltpu.VMEM((BATCHES, NCOL, chunk, width), BF16),
            pltpu.VMEM((BATCHES, NROW, chunk, width), BF16),
            pltpu.SemaphoreType.DMA((6,)),
            pltpu.SemaphoreType.DMA((copies,)),
            pltpu.SemaphoreType.DMA((copies,)),
        ],
        compiler_params=pltpu.CompilerParams(
            collective_id=0, has_side_effects=True, vmem_limit_bytes=60 * 2**20
        ),
        cost_estimate=pl.CostEstimate(flops=2 * slots * TILE * TILE * hidden, bytes_accessed=16 * 2**20, transcendentals=0),
    )(tile_rows, tile_cols, tile_counts, tile_values, out_grad, features, weight)


def solution(mesh):
    placed = (
        P("row", "col", None, None, None),
        P("row", "col", None),
        P("row", "col", None),
        P("row", "col"),
        P(("row", "col"), None),
        P(("row", "col"), None),
        P(),
    )
    return jax.shard_map(
        per_device,
        mesh=mesh,
        in_specs=placed,
        out_specs=(P(("row", "col"), None), P()),
        check_vma=False,
    )
```
